1024 devices in a mesh: layer: 8 (over x, core), row: 8 (over z_lo), col: 16 (over y, z_hi).
Axes of the slice: x: 4, y: 8, z: 16 (z_hi: 2, z_lo: 8; z = z_hi * 8 + z_lo), core: 2. Of those that a mesh axis runs over, the one named last changes fastest.
Arguments:
- phi_row: bfloat16 [16384, 256, 128], P(('layer', 'row', 'col')), may hold values from -6 to 6
- phi_col: bfloat16 [16384, 256, 128], P(('layer', 'row', 'col')), may hold values from -6 to 6
- weights: float32 [16384, 256], P(('layer', 'row', 'col')), may hold values from 0.2 to 300, as said below
- batch_route: int32 [16384, 1], P(('layer', 'row', 'col')), may hold values from 0 to 15; in each aligned block of 16 rows (0 to 15, 16 to 31, ...) at most 2 rows name the same one
- batch_slot: int32 [16384], P(('layer', 'row', 'col')), may hold values from 0 to 7
- ham_pattern: int32 [1024, 8], P(('layer', 'row', 'col')), may hold values 0 or 1
- dens_pattern: int32 [1024, 8], P(('layer', 'row', 'col')), may hold values 0 or 1
Outputs:
- density: bfloat16 [131072, 1024], P(('layer', 'row', 'col'))
- grid_density: float32 [16384, 256], P(('layer', 'row', 'col'))
The draws below stay inside these ranges and needn't reach their ends.
Inputs may be any that keep to these rules, and one draw needn't show every extreme that they name: `batch_route`: batch b targets block row o - (o mod 16) + this value, o its owning device; among the rows of one device each value appears at most 2 times. `weights`: positive.
All inputs are finite; a program needn't handle non-finite values. No bound on the sum of `ham_pattern` or of `dens_pattern` on one device may be relied on, other than what follows from the above.
Results may differ from the reference program's by a relative error of at most 0.014.
Values may be sent and summed in bfloat16 or wider, within the bound.
No kernel may reach another device: no remote copies, remote signals or barrier semaphores. Data moves between devices by JAX's collectives and lax.ppermute only.
A program may use at most 128 MiB of HBM per device.

```python
import math
import jax
import jax.numpy as jnp
import numpy as np
from jax import lax

BLK = 128
SLOTS = 8
NPTS = 256
NBAT = 16
NB = 1024
CAP = 2
NBT = 16384
N_COL = 16


def draw_weights(key, part):
    key = jax.random.fold_in(key, 11)
    point_key, batch_key = jax.random.split(key)
    position = jnp.arange(NBT, dtype=jnp.float32)[:, None] / NBT
    pointwise = jax.random.uniform(point_key, (NBT, NPTS), jnp.float32, 0.5, 1.5)
    per_batch = jnp.exp(jax.random.uniform(batch_key, (NBT, 1), jnp.float32, 0.0, 2.3))
    rising = 1.0 + 2.0 * position
    return pointwise * per_batch * rising


def touch_ends(entries, rng, low, largest):
    spot = [jax.random.randint(jax.random.fold_in(rng, axis), (), 0, length) for axis, length in enumerate(entries.shape)]
    widest = entries.shape.index(max(entries.shape))
    beside = spot[:widest] + [(spot[widest] + 1) % entries.shape[widest]] + spot[widest + 1:]
    return entries.at[tuple(spot)].set(low).at[tuple(beside)].set(largest)


def block_scale(stream_key, extent, shards, low, top_value):
    level = 1.0
    for dim, blocks in shards:
        draws = jax.random.uniform(jax.random.fold_in(jax.random.fold_in(stream_key, 6), dim), (blocks,), jnp.float32, low / len(shards), top_value / len(shards))
        level = level * jnp.repeat(jnp.exp(draws), extent[dim] // blocks).reshape((-1,) + (1,) * (len(extent) - 1 - dim))
    return level


def shared_out(key, own, number, rows, amount, top, most, slope):
    ranking = jax.random.permutation(key, amount)
    heavy_load, usual = portions_of(amount, rows * top, most, slope, True), portions_of(amount, rows * top, most, slope, False)
    places = jnp.arange(amount)

    def named(sizes, turn):
        used = int((sizes > 0).sum())
        fixed = max(1, used // 4)
        moved = fixed + (places - fixed + turn * (used - fixed)) % max(1, amount - fixed)
        return jnp.zeros((amount,), jnp.int32).at[ranking[jnp.where(places < fixed, places, moved)]].set(jnp.asarray(sizes, jnp.int32))

    sizes = jnp.where(number % 4 == 0, named(heavy_load, number // 4), named(usual, number - number // 4 - 1))
    mixed = jax.random.permutation(jax.random.fold_in(own, 3), amount)
    donor, sink = mixed[0:amount // 2 * 2:2], mixed[1:amount // 2 * 2:2]
    slack = jnp.minimum(sizes[donor] - 1, most - sizes[sink]) // 2
    slack = jnp.where((donor == ranking[0]) | (sink == ranking[0]) | (sizes[sink] == 0), 0, jnp.maximum(slack, 0))
    moved = jax.random.randint(jax.random.fold_in(own, 4), (amount // 2,), 0, 1 << 20) % (slack + 1)
    sizes = sizes.at[donor].add(-moved).at[sink].add(moved)
    items = jnp.searchsorted(jnp.cumsum(sizes), jnp.arange(rows * top), side="right").astype(jnp.int32)
    listing = items.reshape(top, rows).T
    listing = listing[jax.random.permutation(jax.random.fold_in(own, 1), rows)]
    turn = jax.random.randint(jax.random.fold_in(own, 2), (rows, 1), 0, top)
    return jnp.take_along_axis(listing, (jnp.arange(top)[None, :] + turn) % top, axis=1)


def portions_of(amount, total, reach, slope, full):
    loads = [(1 << 20) // math.isqrt(standing ** slope) + 1 for standing in range(1, amount + 1)]
    largest = reach if full else min(reach, max(-(-total // amount), total * loads[0] // sum(loads)))
    least = 1 if total - largest >= amount - 1 else 0
    given, spare = [largest] + [least] * (amount - 1), total - largest - least * (amount - 1)
    while spare > 0:
        movable = [i for i in range(1, amount) if given[i] < largest] or [i for i in range(1, amount) if given[i] < reach]
        mass, left = sum([loads[i] for i in movable]), spare
        for i in movable:
            extra = min(reach - given[i], max(1, left * loads[i] // mass), spare)
            given[i] = given[i] + extra
            spare = spare - extra
    return np.array(given)


def noise(key, extent, deviation, limit, cuts=(), kind=jnp.bfloat16):
    level = block_scale(key, extent, cuts, -0.22, 0.18) if cuts else 1.0
    array = jax.random.normal(key, extent, jnp.float32) * deviation * level
    return jnp.minimum(jnp.maximum(array, -limit), limit).astype(kind)


def setup_inputs(seed: int = 0) -> dict:
    keys = jax.random.split(jax.random.key(seed), 8)
    phi_row = noise(keys[0], (NBT, NPTS, BLK), 1.0, 6.0, ((0, 1024),))
    phi_col = noise(keys[1], (NBT, NPTS, BLK), 1.0, 6.0, ((0, 1024),))
    weights = draw_weights(jax.random.fold_in(keys[7], 71), 0)
    batch_route_keys = jax.random.split(jax.random.fold_in(keys[3], 1), NBT // NBAT)
    batch_route_turns = jax.random.permutation(jax.random.fold_in(keys[3], 3), NBT // NBAT)
    batch_route = jax.vmap(lambda own, number: shared_out(jax.random.fold_in(keys[3], 2), own, number, NBAT, N_COL, 1, CAP, 2))(batch_route_keys, batch_route_turns).reshape((NBT, 1))
    batch_slot = touch_ends(jax.random.randint(keys[4], (NBT,), 0, SLOTS), jax.random.fold_in(keys[4], 1), 0, SLOTS - 1).astype(jnp.int32)
    ham_pattern = touch_ends((jax.random.randint(keys[5], (NB, SLOTS), 0, 8) < 7).astype(jnp.int32), jax.random.fold_in(keys[5], 1), 0, 1)
    dens_pattern = touch_ends((jax.random.randint(keys[6], (NB, SLOTS), 0, 4) < 3).astype(jnp.int32), jax.random.fold_in(keys[6], 1), 0, 1)
    return {"phi_row": phi_row, "phi_col": phi_col, "weights": weights, "batch_route": batch_route, "batch_slot": batch_slot, "ham_pattern": ham_pattern, "dens_pattern": dens_pattern}


def column_mask(switch_flags, block_width):
    shaped = jnp.broadcast_to(switch_flags.astype(jnp.float32)[..., :, None], switch_flags.shape + (block_width,))
    return shaped.reshape(switch_flags.shape[:-1] + (switch_flags.shape[-1] * block_width,))

def unit_row(block_width, band_slots):
    columns = jnp.arange(band_slots * block_width, dtype=jnp.int32)[None, :]
    wanted = (jnp.arange(block_width, dtype=jnp.int32) + band_slots // 2 * block_width)[:, None]
    return (columns == wanted).astype(jnp.float32)

def band_rows(window, left_row):
    block_width = left_row.shape[0]
    band_slots = window.shape[0]
    half_band = band_slots // 2
    padded = jnp.pad(window, ((0, 0), (0, 0), (half_band * block_width, half_band * block_width)))
    pieces = [padded[shift_id, :, (band_slots - shift_id) * block_width:(2 * band_slots - shift_id) * block_width] for shift_id in range(band_slots)]
    stacked = jnp.concatenate(pieces, axis=0)
    return jnp.dot(left_row, stacked, preferred_element_type=jnp.float32)

def band_square(matrix):
    band_slots = matrix.shape[2] // matrix.shape[1]
    half_band = band_slots // 2
    padded = jnp.pad(matrix, ((half_band, half_band), (0, 0), (0, 0)))

    def one_row(row_index):
        window = lax.dynamic_slice_in_dim(padded, row_index, band_slots, 0)
        return band_rows(window, matrix[row_index])
    return lax.map(one_row, jnp.arange(matrix.shape[0], dtype=jnp.int32))

def reference(phi_row, phi_col, weights, batch_route, batch_slot, ham_pattern, dens_pattern):
    group_count = NB // N_COL
    per_group = N_COL * NBAT

    def integrate(group_id):
        start_at = (group_id * per_group).astype(jnp.int32)
        rows_a = lax.dynamic_slice_in_dim(phi_row, start_at, per_group, 0).astype(jnp.float32)
        cols_b = lax.dynamic_slice_in_dim(phi_col, start_at, per_group, 0).astype(jnp.float32)
        scales_pts = lax.dynamic_slice_in_dim(weights, start_at, per_group, 0)
        scaled = lax.optimization_barrier((scales_pts[:, :, None] * cols_b).astype(jnp.bfloat16)).astype(jnp.float32)
        contrib = jnp.einsum('bpm,bpn->bmn', rows_a, scaled) / NPTS
        contrib = lax.optimization_barrier(contrib.astype(jnp.bfloat16)).astype(jnp.float32)
        target = lax.dynamic_slice_in_dim(batch_route[:, 0], start_at, per_group, 0) * SLOTS + lax.dynamic_slice_in_dim(batch_slot, start_at, per_group, 0)
        onehot = (target[None, :] == jnp.arange(N_COL * SLOTS, dtype=jnp.int32)[:, None]).astype(jnp.float32)
        summed = jnp.einsum('tb,bmn->tmn', onehot, contrib)
        return summed.reshape(N_COL, SLOTS, BLK, BLK).transpose(0, 2, 1, 3).reshape(N_COL, BLK, SLOTS * BLK)
    hamiltonian = lax.map(integrate, jnp.arange(group_count, dtype=jnp.int32)).reshape(NB, BLK, SLOTS * BLK)
    row_ids = jnp.arange(NB, dtype=jnp.int32)
    col_ids = row_ids[:, None] + jnp.arange(SLOTS, dtype=jnp.int32)[None, :] - SLOTS // 2
    usable = ((col_ids >= 0) & (col_ids < NB)).astype(jnp.int32) * ham_pattern
    hamiltonian = (hamiltonian * column_mask(usable, BLK)[:, None, :]).astype(jnp.bfloat16)
    ham_f32 = hamiltonian.astype(jnp.float32)
    centre = ham_f32[:, :, SLOTS // 2 * BLK:(SLOTS // 2 + 1) * BLK]
    trace_sum = jnp.sum(jnp.trace(centre, axis1=1, axis2=2))
    squares = jnp.sum(ham_f32 * ham_f32)
    mat_order = NB * BLK
    average = trace_sum / mat_order
    spread = jnp.sqrt(squares / mat_order - average * average + 1e-06)
    diag_lift = 0.5 + average / (4.0 * spread)
    scaling = 1.0 / (4.0 * spread)
    identity = unit_row(BLK, SLOTS)
    start = (diag_lift * identity[None] - scaling * ham_f32).astype(jnp.bfloat16)
    dens_mask = column_mask(dens_pattern, BLK)[:, None, :]
    purified_one = (band_square(start) * dens_mask).astype(jnp.bfloat16)
    square_two = band_square(purified_one)
    density = ((2.0 * purified_one.astype(jnp.float32) - square_two) * dens_mask).astype(jnp.bfloat16)
    dblocks = density.reshape(NB, BLK, SLOTS, BLK).transpose(0, 2, 1, 3)

    def grid_values(group_id):
        start_at = (group_id * per_group).astype(jnp.int32)
        rows_a = lax.dynamic_slice_in_dim(phi_row, start_at, per_group, 0).astype(jnp.float32)
        cols_b = lax.dynamic_slice_in_dim(phi_col, start_at, per_group, 0).astype(jnp.float32)
        targets = group_id * N_COL + lax.dynamic_slice_in_dim(batch_route[:, 0], start_at, per_group, 0)
        slot_ids = lax.dynamic_slice_in_dim(batch_slot, start_at, per_group, 0)
        picked = dblocks[targets, slot_ids].astype(jnp.float32)
        partial_value = jnp.einsum('bpm,bmn->bpn', rows_a, picked)
        return lax.optimization_barrier(jnp.sum(partial_value * cols_b, axis=2))
    grid_density = lax.map(grid_values, jnp.arange(group_count, dtype=jnp.int32)).reshape(NBT, NPTS)
    return (density.reshape(NB * BLK, SLOTS * BLK), grid_density)
```

```python
import functools

import jax
import jax.numpy as jnp
from jax import lax
from jax.experimental import pallas as pl
from jax.experimental.pallas import tpu as pltpu
from jax.sharding import Mesh, PartitionSpec as P

BW = 128
SLOTS = 8
HALF = 4
META = 16
WIDE = 9 * BW
LINE = ("layer", "row", "ring")
F32 = jnp.float32
BF16 = jnp.bfloat16
VMEM = pl.BlockSpec(memory_space=pltpu.VMEM)
SMEM = pl.BlockSpec(memory_space=pltpu.SMEM)

REACH = {
    -1: [(-2, s) for s in range(2, 8)] + [(-1, s) for s in range(1, 8)],
    -2: [(-4, s) for s in range(4, 8)] + [(-3, s) for s in range(3, 8)],
    1: [(2, s) for s in range(0, 7)] + [(3, s) for s in range(0, 6)],
    2: [(4, s) for s in range(0, 5)],
}
SIDES = (-1, -2, 1, 2)
OWN = [(r, s) for r in range(2) for s in range(SLOTS)]


def call(kernel, out_shape, in_specs, out_specs, scratch=(), flops=0, moved=0):
    return pl.pallas_call(
        kernel,
        out_shape=out_shape,
        in_specs=in_specs,
        out_specs=out_specs,
        scratch_shapes=list(scratch),
        compiler_params=pltpu.CompilerParams(vmem_limit_bytes=24 * 1024 * 1024),
        cost_estimate=pl.CostEstimate(flops=flops, bytes_accessed=moved, transcendentals=0),
    )


def rows(block):
    return slice(block * BW, (block + 1) * BW)


def integrate(route, slot, w, prow, pcol, out, pos_out, count):
    batches, points, _ = prow.shape
    dests, depth, _ = out.shape
    for t in range(2 * dests):
        count[t] = 0
    w_cols = jnp.concatenate([w[...], jnp.zeros((BW - batches, points), F32)], axis=0).T
    line = lax.broadcasted_iota(jnp.int32, (dests * META, BW), 0)
    named = jnp.where(line % META < 4, line // META * 4 + line % META, -1)
    labels = jnp.zeros((dests * META, BW), F32)
    for b in range(batches):
        t = route[b, 0]
        rank = count[t]
        count[t] = rank + 1
        pos = t * 2 + jnp.minimum(rank, 1)
        pos_out[b] = pos
        labels = jnp.where(named == pos, (slot[b] + 1).astype(F32), labels)
        scaled = (w_cols[:, b : b + 1] * pcol[b].astype(F32)).astype(BF16)
        made = lax.dot_general(
            prow[b], scaled, (((0,), (0,)), ((), ())), preferred_element_type=F32
        )
        at = pl.multiple_of(pos % 4 * BW, BW)
        out[pos // 4, pl.ds(at, BW), :] = (made / points).astype(BF16)
    for d in range(dests):
        out[d, 4 * BW : 4 * BW + META, :] = labels[d * META : (d + 1) * META].astype(BF16)


def accumulate(labels, arrived, ham, dens, out, total):
    total[...] = jnp.zeros_like(total)
    for i in range(4 * arrived.shape[0]):
        label = labels[i]

        @pl.when(label > 0)
        def _():
            at = (i % 4 // 2) * SLOTS + label - 1
            total[at] += arrived[i // 4, rows(i % 4), :].astype(F32)

    for k in range(2 * SLOTS):
        out[rows(k), :] = total[k].astype(BF16)
    line = lax.broadcasted_iota(jnp.int32, (META, BW), 0)
    meta = jnp.zeros((META, BW), F32)
    for s in range(SLOTS):
        meta = jnp.where(line == s, ham[0, s].astype(F32), meta)
        meta = jnp.where(line == s + SLOTS, dens[0, s].astype(F32), meta)
    out[2 * SLOTS * BW :, :] = meta.astype(BF16)


def combine(place, own, other, ham, p1, p2, m1, m2, sums, *, pairs):
    side, pair = place[0], place[1]
    tail = slice(2 * SLOTS * BW, 2 * SLOTS * BW + META)
    meta_own, meta_other = own[tail, :].astype(F32), other[tail, :].astype(F32)
    line = lax.broadcasted_iota(jnp.int32, (SLOTS, BW), 0)
    square = jnp.zeros((BW, BW), F32)
    diag = jnp.zeros((BW, BW), F32)
    masks = []
    for r in range(2):
        mine = side == r
        usable = jnp.where(mine, meta_own[:SLOTS], meta_other[:SLOTS])
        masks.append(jnp.where(mine, meta_own[SLOTS:], meta_other[SLOTS:]))
        column = 2 * pair + r + line - HALF
        usable = jnp.where((column >= 0) & (column < 2 * pairs), usable, 0.0)
        for s in range(SLOTS):
            k = r * SLOTS + s
            value = own[rows(k), :].astype(F32) + other[rows(k), :].astype(F32)
            block = (value * usable[s : s + 1, :]).astype(BF16)
            ham[rows(k), :] = block
            wide = block.astype(F32)
            square += wide * wide
            if s == HALF:
                diag += wide
    eye = lax.broadcasted_iota(jnp.int32, (BW, BW), 0) == lax.broadcasted_iota(
        jnp.int32, (BW, BW), 1
    )
    trace_sum = jnp.sum(jnp.where(eye, diag, 0.0), axis=(0, 1), keepdims=True)
    square_sum = jnp.sum(square, axis=(0, 1), keepdims=True)
    sums[...] = jnp.where(line == 0, trace_sum, square_sum)
    meta = jnp.concatenate(masks, axis=0).astype(BF16)
    ham[tail, :] = meta
    for piece, towards in ((p1, 1), (p2, 2), (m1, -1), (m2, -2)):
        send_piece(ham, piece, towards)
        piece[len(REACH[-towards]) * BW :, :] = meta


def send_piece(source, piece, towards):
    for i, (b, s) in enumerate(REACH[-towards]):
        r = b + 2 * towards
        piece[rows(i), :] = source[rows(r * SLOTS + s), :]


def fill(right, ours, near, make):
    places = [(ours, i, b, s) for i, (b, s) in enumerate(OWN)]
    for piece, which in zip(near, SIDES):
        places += [(piece, i, b, s) for i, (b, s) in enumerate(REACH[which])]
    given = set()
    for piece, i, b, s in places:
        c = b + s - HALF
        given.add((b, c))
        right[rows(b + HALF), rows(c + HALF)] = make(piece, i, b, s)
    for b in range(-HALF, HALF + 1):
        for c in range(-HALF, HALF + 1):
            if (b, c) not in given:
                right[rows(b + HALF), rows(c + HALF)] = jnp.zeros((BW, BW), BF16)


def square_pair(right):
    left = right[HALF * BW : (HALF + 2) * BW, :]
    for j in range(3):
        span = slice(j * 3 * BW, (j + 1) * 3 * BW)
        yield j, jnp.dot(left, right[:, span], preferred_element_type=F32)


def first_square(ham, a1, a2, b1, b2, out, p1, p2, m1, m2, right):
    fill(right, ham, (a1, a2, b1, b2), lambda piece, i, b, s: piece[rows(i), :])
    for j, made in square_pair(right):
        for i in range(3):
            for r in range(2):
                s = 3 * j + i - r
                if 0 <= s < SLOTS:
                    out[rows(r * SLOTS + s), :] = made[rows(r), rows(i)].astype(BF16)
    for piece, towards in ((p1, 1), (p2, 2), (m1, -1), (m2, -2)):
        send_piece(out, piece, towards)


def second_square(
    place, labels, sums, ham, ha1, ha2, hb1, hb2, sq, ga1, ga2, gb1, gb2,
    density, answers, right, blocks, *, order,
):
    side = place[0]
    average = sums[0:1, :] / order
    spread = jnp.sqrt(sums[1:2, :] / order - average * average + 1e-06)
    lift = 0.5 + average / (4.0 * spread)
    scaling = 1.0 / (4.0 * spread)
    unit, linear, quadratic = lift * lift, 2.0 * lift * scaling, scaling * scaling
    eye = lax.broadcasted_iota(jnp.int32, (BW, BW), 0) == lax.broadcasted_iota(
        jnp.int32, (BW, BW), 1
    )
    unit_block = jnp.where(eye, jnp.broadcast_to(unit, (BW, BW)), 0.0)
    squares = {id(ham): sq, id(ha1): ga1, id(ha2): ga2, id(hb1): gb1, id(hb2): gb2}
    masks = {}
    for piece in (ham, ha1, ha2, hb1, hb2):
        masks[id(piece)] = piece[piece.shape[0] - META :, :].astype(F32)

    def make(piece, i, b, s):
        line = b % 2 * SLOTS + s
        value = quadratic * squares[id(piece)][rows(i), :].astype(F32)
        value = value - linear * piece[rows(i), :].astype(F32)
        if s == HALF:
            value = value + unit_block
        return (value * masks[id(piece)][line : line + 1, :]).astype(BF16)

    fill(right, ham, (ha1, ha2, hb1, hb2), make)
    mask = masks[id(ham)]
    for j, made in square_pair(right):
        for i in range(3):
            for r in range(2):
                s = 3 * j + i - r
                if 0 <= s < SLOTS:
                    k = r * SLOTS + s
                    first = right[rows(HALF + r), rows(3 * j + i)].astype(F32)
                    value = (2.0 * first - made[rows(r), rows(i)]) * mask[k : k + 1, :]
                    blocks[k] = value.astype(BF16)
    for s in range(SLOTS):
        density[:, rows(s)] = blocks[side * SLOTS + s]
    for i in range(4 * answers.shape[0]):
        label = jnp.maximum(labels[i], 1)
        answers[i // 4, rows(i % 4), :] = blocks[(i % 4 // 2) * SLOTS + label - 1]


def on_grid(pos, returned, prow, pcol, out):
    batches, points, _ = prow.shape
    lane = lax.broadcasted_iota(jnp.int32, (points, BW), 1)
    values = jnp.zeros((points, BW), F32)
    for b in range(batches):
        at = pl.multiple_of(pos[b] % 4 * BW, BW)
        block = returned[pos[b] // 4, pl.ds(at, BW), :]
        partial = jnp.dot(prow[b], block, preferred_element_type=F32) * pcol[b].astype(F32)
        values = jnp.where(lane == b, jnp.sum(partial, axis=1, keepdims=True), values)
    out[...] = values.T[:batches, :]


def moved_along(piece, steps):
    count = lax.axis_size(LINE)
    first, last = max(0, -steps), min(count, count - steps)
    return lax.ppermute(piece, LINE, [(i, i + steps) for i in range(first, last)])


def summed_over_pairs(sums):
    for axis in ("ring", "row", "layer"):
        size = lax.axis_size(axis)
        step = 1
        while step < size:
            sums = sums + lax.ppermute(sums, axis, [(i, i ^ step) for i in range(size)])
            step *= 2
    return sums


def shards(phi_row, phi_col, weights, batch_route, batch_slot, ham_pattern, dens_pattern):
    batches, points, _ = phi_row.shape
    dests = lax.axis_size("ring")
    pairs = lax.axis_size(LINE)
    place = jnp.stack([lax.axis_index("side"), lax.axis_index(LINE)]).astype(jnp.int32)
    depth = 4 * BW + META

    def shape(*dims, kind=BF16):
        return jax.ShapeDtypeStruct(dims, kind)

    outgoing, position = call(
        integrate,
        (shape(dests, depth, BW), shape(batches, kind=jnp.int32)),
        [SMEM, SMEM, VMEM, VMEM, VMEM],
        (VMEM, SMEM),
        [pltpu.SMEM((2 * dests,), jnp.int32)],
        flops=2 * batches * points * BW * BW,
        moved=6 << 20,
    )(batch_route, batch_slot, weights, phi_row, phi_col)
    arrived = lax.all_to_all(outgoing, "ring", split_axis=0, concat_axis=0, tiled=True)
    labels = arrived[:, 4 * BW : 4 * BW + 4, 0].astype(jnp.int32).reshape(4 * dests)

    whole = 2 * SLOTS * BW + META
    part = call(
        accumulate,
        shape(whole, BW),
        [SMEM, VMEM, SMEM, SMEM],
        VMEM,
        [pltpu.VMEM((2 * SLOTS, BW, BW), F32)],
        moved=4 << 20,
    )(labels, arrived, ham_pattern, dens_pattern)
    other = lax.ppermute(part, "side", [(0, 1), (1, 0)])

    size = {t: len(REACH[-t]) * BW for t in (1, 2, -1, -2)}
    ham, p1, p2, m1, m2, sums = call(
        functools.partial(combine, pairs=pairs),
        (shape(whole, BW),)
        + tuple(shape(size[t] + META, BW) for t in (1, 2, -1, -2))
        + (shape(SLOTS, BW, kind=F32),),
        [SMEM, VMEM, VMEM],
        (VMEM,) * 6,
        moved=4 << 20,
    )(place, part, other)
    near = [moved_along(p, t) for p, t in ((p1, 1), (p2, 2), (m1, -1), (m2, -2))]
    sums = summed_over_pairs(sums)

    sq, p1, p2, m1, m2 = call(
        first_square,
        (shape(2 * SLOTS * BW, BW),) + tuple(shape(size[t], BW) for t in (1, 2, -1, -2)),
        [VMEM] * 5,
        (VMEM,) * 5,
        [pltpu.VMEM((WIDE, WIDE), BF16)],
        flops=4 * BW * WIDE * WIDE,
        moved=4 << 20,
    )(ham, *near)
    near_sq = [moved_along(p, t) for p, t in ((p1, 1), (p2, 2), (m1, -1), (m2, -2))]

    density, answers = call(
        functools.partial(second_square, order=2 * pairs * BW),
        (shape(BW, SLOTS * BW), shape(dests, 4 * BW, BW)),
        [SMEM, SMEM] + [VMEM] * 11,
        (VMEM, VMEM),
        [pltpu.VMEM((WIDE, WIDE), BF16), pltpu.VMEM((2 * SLOTS, BW, BW), BF16)],
        flops=4 * BW * WIDE * WIDE,
        moved=6 << 20,
    )(place, labels, sums, ham, *near, sq, *near_sq)
    returned = lax.all_to_all(answers, "ring", split_axis=0, concat_axis=0, tiled=True)

    grid_density = call(
        on_grid,
        shape(batches, points, kind=F32),
        [SMEM, VMEM, VMEM, VMEM],
        VMEM,
        flops=2 * batches * points * BW * BW,
        moved=6 << 20,
    )(position, returned, phi_row, phi_col)
    return (density, grid_density)


def solution(mesh):
    layer, row, col = (mesh.shape[a] for a in ("layer", "row", "col"))
    split = Mesh(
        mesh.devices.reshape(layer, row, col // 2, 2), ("layer", "row", "ring", "side")
    )
    axes = ("layer", "row", "ring", "side")
    in_specs = (
        P(axes, None, None),
        P(axes, None, None),
        P(axes, None),
        P(axes, None),
        P(axes),
        P(axes, None),
        P(axes, None),
    )
    out_specs = (P(axes, None), P(axes, None))
    return jax.shard_map(
        shards, mesh=split, in_specs=in_specs, out_specs=out_specs, check_vma=False
    )
```

```python
import functools

import jax
import jax.numpy as jnp
from jax import lax
from jax.experimental import pallas as pl
from jax.experimental.pallas import tpu as pltpu
from jax.sharding import Mesh, PartitionSpec as P

BW = 128
SLOTS = 8
HALF = 4
META = 16
CARRIED = 32
WIDE = 9 * BW
LINE = ("layer", "row", "ring")
F32 = jnp.float32
BF16 = jnp.bfloat16
VMEM = pl.BlockSpec(memory_space=pltpu.VMEM)
SMEM = pl.BlockSpec(memory_space=pltpu.SMEM)

REACH = {
    -1: [(-2, s) for s in range(2, 8)] + [(-1, s) for s in range(1, 8)],
    -2: [(-4, s) for s in range(4, 8)] + [(-3, s) for s in range(3, 8)],
    1: [(2, s) for s in range(0, 7)] + [(3, s) for s in range(0, 6)],
    2: [(4, s) for s in range(0, 5)],
}
SIDES = (-1, -2, 1, 2)
OWN = [(r, s) for r in range(2) for s in range(SLOTS)]


def call(kernel, out_shape, in_specs, out_specs, scratch=(), flops=0, moved=0):
    return pl.pallas_call(
        kernel,
        out_shape=out_shape,
        in_specs=in_specs,
        out_specs=out_specs,
        scratch_shapes=list(scratch),
        compiler_params=pltpu.CompilerParams(vmem_limit_bytes=24 * 1024 * 1024),
        cost_estimate=pl.CostEstimate(flops=flops, bytes_accessed=moved, transcendentals=0),
    )


def rows(block):
    return slice(block * BW, (block + 1) * BW)


def integrate(place, route, slot, w, prow, pcol, out_other, out_own, pos_out, made, count):
    batches, points, _ = prow.shape
    dests = out_own.shape[0]
    for t in range(2 * dests):
        count[t] = 0
    w_cols = jnp.concatenate([w[...], jnp.zeros((BW - batches, points), F32)], axis=0).T
    line = lax.broadcasted_iota(jnp.int32, (dests * META, BW), 0)
    named = jnp.where(line % META < 4, line // META * 4 + line % META, -1)
    labels = jnp.zeros((dests * META, BW), F32)
    for b in range(batches):
        t = route[b]
        rank = count[t]
        count[t] = rank + 1
        pos = t * 2 + jnp.minimum(rank, 1)
        pos_out[b] = pos
        labels = jnp.where(named == pos, (slot[b] + 1).astype(F32), labels)
    labels = labels.astype(BF16)
    for d in range(dests):
        out_own[d, 2 * BW :, :] = labels[d * META : (d + 1) * META]
        out_other[d, 2 * BW :, :] = labels[d * META : (d + 1) * META]
    for b in range(batches):
        scaled = (w_cols[:, b : b + 1] * pcol[b].astype(F32)).astype(BF16)
        value = lax.dot_general(
            prow[b], scaled, (((0,), (0,)), ((), ())), preferred_element_type=F32
        )
        made[b] = (value / points).astype(BF16)
    for b in range(batches):
        pos = pos_out[b]
        mine = pos // 2 % 2 == place[0]
        at = pl.multiple_of(pos % 2 * BW, BW)

        @pl.when(mine)
        def _():
            out_own[pos // 4, pl.ds(at, BW), :] = made[b]

        @pl.when(jnp.logical_not(mine))
        def _():
            out_other[pos // 4, pl.ds(at, BW), :] = made[b]


def accumulate(labels, arrived, out, total):
    total[...] = jnp.zeros_like(total)
    for i in range(2 * arrived.shape[0]):
        label = labels[i]

        @pl.when(label > 0)
        def _():
            total[label - 1] += arrived[i // 2, rows(i % 2), :].astype(F32)

    for s in range(SLOTS):
        out[rows(s), :] = total[s].astype(out.dtype)


def combine(place, ham_pattern, dens_pattern, own, other, ham, sums, *, pairs):
    column = 2 * place[1] + place[0] - HALF
    line = lax.broadcasted_iota(jnp.int32, (META, BW), 0)
    meta = jnp.zeros((META, BW), F32)
    square = jnp.zeros((BW, BW), F32)
    for s in range(SLOTS):
        meta = jnp.where(line == s, dens_pattern[0, s].astype(F32), meta)
        inside = (column + s >= 0) & (column + s < 2 * pairs)
        usable = jnp.where(inside, ham_pattern[0, s], 0).astype(F32)
        value = own[rows(s), :] + other[rows(s), :].astype(F32)
        block = (value * usable).astype(BF16)
        ham[rows(s), :] = block
        wide = block.astype(F32)
        square += wide * wide
        if s == HALF:
            diag = wide
    eye = lax.broadcasted_iota(jnp.int32, (BW, BW), 0) == lax.broadcasted_iota(
        jnp.int32, (BW, BW), 1
    )
    trace_sum = jnp.sum(jnp.where(eye, diag, 0.0), axis=(0, 1), keepdims=True)
    square_sum = jnp.sum(square, axis=(0, 1), keepdims=True)
    sums[...] = jnp.where(line[:SLOTS] == 0, trace_sum, square_sum)
    ham[SLOTS * BW :, :] = meta.astype(BF16)


def carried(sums):
    high = sums.astype(BF16).astype(F32)
    middle = (sums - high).astype(BF16).astype(F32)
    low = sums - high - middle
    return jnp.concatenate([high, middle, low, jnp.zeros_like(low)], axis=0).astype(BF16)


def brought(piece):
    parts = piece[piece.shape[0] - CARRIED :, :].astype(F32)
    return parts[:SLOTS] + parts[SLOTS : 2 * SLOTS] + parts[2 * SLOTS : 3 * SLOTS]


def spread(place, sums, own, other, ham, *outs):
    side, size = place[0], SLOTS * BW
    pieces, sums_out = outs[:4], outs[4]
    sums_out[...] = sums[...]
    ham[pl.ds(pl.multiple_of(side * size, size), size), :] = own[:size, :]
    ham[pl.ds(pl.multiple_of((1 - side) * size, size), size), :] = other[:size, :]
    mine, others = own[size:, :].astype(F32), other[size : size + META, :].astype(F32)
    masks = [jnp.where(side == r, mine, others)[:SLOTS] for r in range(2)]
    meta = jnp.concatenate(masks, axis=0).astype(BF16)
    ham[2 * size :, :] = meta
    deal(place, ham, pieces, meta)


def send_piece(source, piece, towards):
    for i, (b, s) in enumerate(REACH[-towards]):
        r = b + 2 * towards
        piece[rows(i), :] = source[rows(r * SLOTS + s), :]


def by_turn(place, step, act):
    behind = place[1] // step % 2
    pl.when(behind == 0)(lambda: act(step, -step))
    pl.when(behind != 0)(lambda: act(-step, step))


def deal(place, source, pieces, tail):
    for step, early, late in ((1, *pieces[:2]), (2, *pieces[2:])):

        def act(first, second, early=early, late=late):
            send_piece(source, early, first)
            send_piece(source, late, second)

        by_turn(place, step, act)
    for piece in pieces:
        piece[piece.shape[0] - tail.shape[0] :, :] = tail


def fill(place, right, ours, near, make):
    given = {(b, b + s - HALF) for b, s in OWN + sum(REACH.values(), [])}
    for b in range(-HALF, HALF + 1):
        for c in range(-HALF, HALF + 1):
            if (b, c) not in given:
                right[rows(b + HALF), rows(c + HALF)] = jnp.zeros((BW, BW), BF16)

    def lay(piece, blocks):
        for i, (b, s) in enumerate(blocks):
            right[rows(b + HALF), rows(b + s)] = make(piece, i, b, s)

    lay(ours, OWN)

    for step, early, late in ((1, *near[:2]), (2, *near[2:])):

        def act(first, second, early=early, late=late):
            lay(early, REACH[first])
            lay(late, REACH[second])

        by_turn(place, step, act)


def square_pair(right):
    left = right[HALF * BW : (HALF + 2) * BW, :]
    for j in range(3):
        span = slice(j * 3 * BW, (j + 1) * 3 * BW)
        yield j, jnp.dot(left, right[:, span], preferred_element_type=F32)


def first_square(place, sums, ham, *refs):
    near, out, pieces, right = refs[:4], refs[4], refs[5:9], refs[9]
    fill(place, right, ham, near, lambda piece, i, b, s: piece[rows(i), :])
    for j, made in square_pair(right):
        for i in range(3):
            for r in range(2):
                s = 3 * j + i - r
                if 0 <= s < SLOTS:
                    out[rows(r * SLOTS + s), :] = made[rows(r), rows(i)].astype(BF16)
    deal(place, out, pieces, carried(sums[...]))


def second_square(place, labels_own, labels_other, sums, ham, *refs, order):
    near, sq, near_sq = refs[:4], refs[4], refs[5:9]
    density, answers, right, blocks = refs[9:]
    side = place[0]
    total = sums[...] + brought(near_sq[0]) + brought(near_sq[1]) + brought(near_sq[2])
    average = total[0:1, :] / order
    spread = jnp.sqrt(total[1:2, :] / order - average * average + 1e-06)
    lift = 0.5 + average / (4.0 * spread)
    scaling = 1.0 / (4.0 * spread)
    unit, linear, quadratic = lift * lift, 2.0 * lift * scaling, scaling * scaling
    eye = lax.broadcasted_iota(jnp.int32, (BW, BW), 0) == lax.broadcasted_iota(
        jnp.int32, (BW, BW), 1
    )
    unit_block = jnp.where(eye, jnp.broadcast_to(unit, (BW, BW)), 0.0)
    squares = {id(ham): sq} | {id(h): g for h, g in zip(near, near_sq)}
    masks = {}
    for piece in (ham, *near):
        masks[id(piece)] = piece[piece.shape[0] - META :, :].astype(F32)

    def make(piece, i, b, s):
        line = b % 2 * SLOTS + s
        value = quadratic * squares[id(piece)][rows(i), :].astype(F32)
        value = value - linear * piece[rows(i), :].astype(F32)
        if s == HALF:
            value = value + unit_block
        return (value * masks[id(piece)][line : line + 1, :]).astype(BF16)

    fill(place, right, ham, near, make)
    mask = masks[id(ham)]
    for j, made in square_pair(right):
        for i in range(3):
            for r in range(2):
                s = 3 * j + i - r
                if 0 <= s < SLOTS:
                    k = r * SLOTS + s
                    first = right[rows(HALF + r), rows(3 * j + i)].astype(F32)
                    value = (2.0 * first - made[rows(r), rows(i)]) * mask[k : k + 1, :]
                    blocks[k] = value.astype(BF16)
    for s in range(SLOTS):
        density[:, rows(s)] = blocks[side * SLOTS + s]
    for labels, row in ((labels_own, side), (labels_other, 1 - side)):
        for i in range(2 * answers.shape[0]):
            label = jnp.maximum(labels[i], 1)
            at = pl.multiple_of((row * 2 + i % 2) * BW, BW)
            answers[i // 2, pl.ds(at, BW), :] = blocks[row * SLOTS + label - 1]


def on_grid(pos, returned, prow, pcol, out):
    batches, points, _ = prow.shape
    lane = lax.broadcasted_iota(jnp.int32, (points, BW), 1)
    values = jnp.zeros((points, BW), F32)
    for b in range(batches):
        at = pl.multiple_of(pos[b] % 4 * BW, BW)
        block = returned[pos[b] // 4, pl.ds(at, BW), :]
        partial = jnp.dot(prow[b], block, preferred_element_type=F32) * pcol[b].astype(F32)
        values = jnp.where(lane == b, jnp.sum(partial, axis=1, keepdims=True), values)
    out[...] = values.T[:batches, :]


def exchanged(pieces):
    count = lax.axis_size(LINE)
    got = []
    for piece, step, turn in zip(pieces, (1, 1, 2, 2), (0, 1, 0, 1)):
        hops = [(i, (i + step) % count) for i in range(count) if i // step % 2 == turn]
        got.append(lax.ppermute(piece, LINE, hops + [(b, a) for a, b in hops]))
    return got


def added_over(sums, *rounds):
    for axis, step in rounds:
        size = lax.axis_size(axis)
        if step < size:
            sums = sums + lax.ppermute(sums, axis, [(i, i ^ step) for i in range(size)])
    return sums


ROUNDS = (
    (("layer", 1), ("layer", 2), ("layer", 4), ("ring", 4), ("row", 1), ("row", 2), ("row", 4)),
    (("side", 1),),
)


def shards(phi_row, phi_col, weights, batch_route, batch_slot, ham_pattern, dens_pattern):
    batches, points, _ = phi_row.shape
    dests = lax.axis_size("ring")
    pairs = lax.axis_size(LINE)
    side = lax.axis_index("side")
    place = jnp.stack([side, lax.axis_index(LINE)]).astype(jnp.int32)
    depth = 2 * BW + META

    def shape(*dims, kind=BF16):
        return jax.ShapeDtypeStruct(dims, kind)

    out_other, out_own, position = call(
        integrate,
        (shape(dests, depth, BW), shape(dests, depth, BW), shape(batches, kind=jnp.int32)),
        [SMEM, SMEM, SMEM, VMEM, VMEM, VMEM],
        (VMEM, VMEM, SMEM),
        [
            pltpu.VMEM((batches, BW, BW), BF16),
            pltpu.SMEM((2 * dests,), jnp.int32),
        ],
        flops=2 * batches * points * BW * BW,
        moved=6 << 20,
    )(place, batch_route.reshape(batches), batch_slot, weights, phi_row, phi_col)

    def received(outgoing, parity, kind):
        arrived = lax.all_to_all(outgoing, "ring", split_axis=0, concat_axis=0, tiled=True)
        labels = arrived[:, 2 * BW : 2 * BW + 4, 0].astype(jnp.int32)
        labels = jnp.where(parity == 0, labels[:, :2], labels[:, 2:]).reshape(2 * dests)
        part = call(
            accumulate,
            shape(SLOTS * BW, BW, kind=kind),
            [SMEM, VMEM],
            VMEM,
            [pltpu.VMEM((SLOTS, BW, BW), F32)],
            moved=2 << 20,
        )(labels, arrived)
        return labels, part

    swap = [(0, 1), (1, 0)]
    labels_other, for_other = received(out_other, 1 - side, BF16)
    from_other = lax.ppermute(for_other, "side", swap)
    labels_own, part = received(out_own, side, F32)

    row_shape = shape(SLOTS * BW + META, BW)
    sums_shape = shape(SLOTS, BW, kind=F32)
    ham_own, sums = call(
        functools.partial(combine, pairs=pairs),
        (row_shape, sums_shape),
        [SMEM, SMEM, SMEM, VMEM, VMEM],
        (VMEM, VMEM),
        moved=2 << 20,
    )(place, ham_pattern, dens_pattern, part, from_other)
    ham_other = lax.ppermute(ham_own, "side", swap)
    sums = added_over(sums, *ROUNDS[0])
    sizes = [len(REACH[t]) * BW for t in (-1, -1, -2, -2)]
    ham, *pieces, sums = call(
        spread,
        (shape(2 * SLOTS * BW + META, BW),)
        + tuple(shape(n + META, BW) for n in sizes)
        + (sums_shape,),
        [SMEM, VMEM, VMEM, VMEM],
        (VMEM,) * 6,
        moved=4 << 20,
    )(place, sums, ham_own, ham_other)
    near = exchanged(pieces)
    sums = added_over(sums, *ROUNDS[1])

    sq, *pieces = call(
        first_square,
        (shape(2 * SLOTS * BW, BW),) + tuple(shape(n + CARRIED, BW) for n in sizes),
        [SMEM] + [VMEM] * 6,
        (VMEM,) * 5,
        [pltpu.VMEM((WIDE, WIDE), BF16)],
        flops=4 * BW * WIDE * WIDE,
        moved=4 << 20,
    )(place, sums, ham, *near)
    near_sq = exchanged(pieces)

    density, answers = call(
        functools.partial(second_square, order=2 * pairs * BW),
        (shape(BW, SLOTS * BW), shape(dests, 4 * BW, BW)),
        [SMEM] * 3 + [VMEM] * 11,
        (VMEM, VMEM),
        [pltpu.VMEM((WIDE, WIDE), BF16), pltpu.VMEM((2 * SLOTS, BW, BW), BF16)],
        flops=4 * BW * WIDE * WIDE,
        moved=6 << 20,
    )(place, labels_own, labels_other, sums, ham, *near, sq, *near_sq)
    returned = lax.all_to_all(answers, "ring", split_axis=0, concat_axis=0, tiled=True)

    grid_density = call(
        on_grid,
        shape(batches, points, kind=F32),
        [SMEM, VMEM, VMEM, VMEM],
        VMEM,
        flops=2 * batches * points * BW * BW,
        moved=6 << 20,
    )(position, returned, phi_row, phi_col)
    return (density, grid_density)


def solution(mesh):
    layer, row, col = (mesh.shape[a] for a in ("layer", "row", "col"))
    split = Mesh(
        mesh.devices.reshape(layer, row, col // 2, 2), ("layer", "row", "ring", "side")
    )
    axes = ("layer", "row", "ring", "side")
    in_specs = (
        P(axes, None, None),
        P(axes, None, None),
        P(axes, None),
        P(axes, None),
        P(axes),
        P(axes, None),
        P(axes, None),
    )
    out_specs = (P(axes, None), P(axes, None))
    return jax.shard_map(
        shards, mesh=split, in_specs=in_specs, out_specs=out_specs, check_vma=False
    )
```

```python
import functools

import jax
import jax.numpy as jnp
from jax import lax
from jax.experimental import pallas as pl
from jax.experimental.pallas import tpu as pltpu
from jax.sharding import Mesh, PartitionSpec as P

BW = 128
SLOTS = 8
HALF = 4
META = 16
CARRIED = 32
WIDE = 9 * BW
LINE = ("layer", "row", "ring")
F32 = jnp.float32
BF16 = jnp.bfloat16
VMEM = pl.BlockSpec(memory_space=pltpu.VMEM)
SMEM = pl.BlockSpec(memory_space=pltpu.SMEM)

REACH = {
    -1: [(-2, s) for s in range(2, 8)] + [(-1, s) for s in range(1, 8)],
    -2: [(-4, s) for s in range(4, 8)] + [(-3, s) for s in range(3, 8)],
    1: [(2, s) for s in range(0, 7)] + [(3, s) for s in range(0, 6)],
    2: [(4, s) for s in range(0, 5)],
}
SIDES = (-1, -2, 1, 2)
OWN = [(r, s) for r in range(2) for s in range(SLOTS)]


def call(kernel, out_shape, in_specs, out_specs, scratch=(), flops=0, moved=0):
    return pl.pallas_call(
        kernel,
        out_shape=out_shape,
        in_specs=in_specs,
        out_specs=out_specs,
        scratch_shapes=list(scratch),
        compiler_params=pltpu.CompilerParams(vmem_limit_bytes=24 * 1024 * 1024),
        cost_estimate=pl.CostEstimate(flops=flops, bytes_accessed=moved, transcendentals=0),
    )


def rows(block):
    return slice(block * BW, (block + 1) * BW)


def integrate(place, route, slot, w, prow, pcol, out_other, out_own, pos_out, made, count):
    batches, points, _ = prow.shape
    dests = out_own.shape[0]
    for t in range(2 * dests):
        count[t] = 0
    w_cols = jnp.concatenate([w[...], jnp.zeros((BW - batches, points), F32)], axis=0).T
    line = lax.broadcasted_iota(jnp.int32, (dests * META, BW), 0)
    named = jnp.where(line % META < 4, line // META * 4 + line % META, -1)
    labels = jnp.zeros((dests * META, BW), F32)
    for b in range(batches):
        t = route[b]
        rank = count[t]
        count[t] = rank + 1
        pos = t * 2 + jnp.minimum(rank, 1)
        pos_out[b] = pos
        labels = jnp.where(named == pos, (slot[b] + 1).astype(F32), labels)
    labels = labels.astype(BF16)
    for d in range(dests):
        out_own[d, 2 * BW :, :] = labels[d * META : (d + 1) * META]
        out_other[d, 2 * BW :, :] = labels[d * META : (d + 1) * META]
    for b in range(batches):
        scaled = (w_cols[:, b : b + 1] * pcol[b].astype(F32)).astype(BF16)
        value = lax.dot_general(
            prow[b], scaled, (((0,), (0,)), ((), ())), preferred_element_type=F32
        )
        made[b] = (value / points).astype(BF16)
    for b in range(batches):
        pos = pos_out[b]
        mine = pos // 2 % 2 == place[0]
        at = pl.multiple_of(pos % 2 * BW, BW)

        @pl.when(mine)
        def _():
            out_own[pos // 4, pl.ds(at, BW), :] = made[b]

        @pl.when(jnp.logical_not(mine))
        def _():
            out_other[pos // 4, pl.ds(at, BW), :] = made[b]


def accumulate(labels, arrived, out, total):
    total[...] = jnp.zeros_like(total)
    for i in range(2 * arrived.shape[0]):
        label = labels[i]

        @pl.when(label > 0)
        def _():
            total[label - 1] += arrived[i // 2, rows(i % 2), :].astype(F32)

    for s in range(SLOTS):
        out[rows(s), :] = total[s].astype(out.dtype)


def combine(place, ham_pattern, dens_pattern, own, other, ham, sums, *, pairs):
    column = 2 * place[1] + place[0] - HALF
    line = lax.broadcasted_iota(jnp.int32, (META, BW), 0)
    meta = jnp.zeros((META, BW), F32)
    square = jnp.zeros((BW, BW), F32)
    for s in range(SLOTS):
        meta = jnp.where(line == s, dens_pattern[0, s].astype(F32), meta)
        inside = (column + s >= 0) & (column + s < 2 * pairs)
        usable = jnp.where(inside, ham_pattern[0, s], 0).astype(F32)
        value = own[rows(s), :] + other[rows(s), :].astype(F32)
        block = (value * usable).astype(BF16)
        ham[rows(s), :] = block
        wide = block.astype(F32)
        square += wide * wide
        if s == HALF:
            diag = wide
    eye = lax.broadcasted_iota(jnp.int32, (BW, BW), 0) == lax.broadcasted_iota(
        jnp.int32, (BW, BW), 1
    )
    trace_sum = jnp.sum(jnp.where(eye, diag, 0.0), axis=(0, 1), keepdims=True)
    square_sum = jnp.sum(square, axis=(0, 1), keepdims=True)
    sums[...] = jnp.where(line[:SLOTS] == 0, trace_sum, square_sum)
    ham[SLOTS * BW :, :] = meta.astype(BF16)


def carried(sums):
    high = sums.astype(BF16).astype(F32)
    middle = (sums - high).astype(BF16).astype(F32)
    low = sums - high - middle
    return jnp.concatenate([high, middle, low, jnp.zeros_like(low)], axis=0).astype(BF16)


def brought(piece):
    parts = piece[piece.shape[0] - CARRIED :, :].astype(F32)
    return parts[:SLOTS] + parts[SLOTS : 2 * SLOTS] + parts[2 * SLOTS : 3 * SLOTS]


def hold(sums, source, out):
    size = source.shape[0]
    out[:size, :] = source[...]
    out[size:, :] = carried(sums[...])


def spread(place, sums, own, other, ham, *outs):
    side, size = place[0], SLOTS * BW
    pieces, sums_out = outs[:4], outs[4]
    sums_out[...] = sums[...] + brought(other)
    ham[pl.ds(pl.multiple_of(side * size, size), size), :] = own[:size, :]
    ham[pl.ds(pl.multiple_of((1 - side) * size, size), size), :] = other[:size, :]
    mine, others = own[size:, :].astype(F32), other[size : size + META, :].astype(F32)
    masks = [jnp.where(side == r, mine, others)[:SLOTS] for r in range(2)]
    meta = jnp.concatenate(masks, axis=0).astype(BF16)
    ham[2 * size :, :] = meta
    deal(place, ham, pieces, meta)


def send_piece(source, piece, towards):
    for i, (b, s) in enumerate(REACH[-towards]):
        r = b + 2 * towards
        piece[rows(i), :] = source[rows(r * SLOTS + s), :]


def by_turn(place, step, act):
    behind = place[1] // step % 2
    pl.when(behind == 0)(lambda: act(step, -step))
    pl.when(behind != 0)(lambda: act(-step, step))


def deal(place, source, pieces, tail):
    for step, early, late in ((1, *pieces[:2]), (2, *pieces[2:])):

        def act(first, second, early=early, late=late):
            send_piece(source, early, first)
            send_piece(source, late, second)

        by_turn(place, step, act)
    for piece in pieces:
        piece[piece.shape[0] - tail.shape[0] :, :] = tail


def fill(place, right, ours, near, make):
    given = {(b, b + s - HALF) for b, s in OWN + sum(REACH.values(), [])}
    for b in range(-HALF, HALF + 1):
        for c in range(-HALF, HALF + 1):
            if (b, c) not in given:
                right[rows(b + HALF), rows(c + HALF)] = jnp.zeros((BW, BW), BF16)

    def lay(piece, blocks):
        for i, (b, s) in enumerate(blocks):
            right[rows(b + HALF), rows(b + s)] = make(piece, i, b, s)

    lay(ours, OWN)

    for step, early, late in ((1, *near[:2]), (2, *near[2:])):

        def act(first, second, early=early, late=late):
            lay(early, REACH[first])
            lay(late, REACH[second])

        by_turn(place, step, act)


def square_pair(right):
    left = right[HALF * BW : (HALF + 2) * BW, :]
    for j in range(3):
        span = slice(j * 3 * BW, (j + 1) * 3 * BW)
        yield j, jnp.dot(left, right[:, span], preferred_element_type=F32)


def first_square(place, sums, ham, *refs):
    near, out, pieces, right = refs[:4], refs[4], refs[5:9], refs[9]
    fill(place, right, ham, near, lambda piece, i, b, s: piece[rows(i), :])
    for j, made in square_pair(right):
        for i in range(3):
            for r in range(2):
                s = 3 * j + i - r
                if 0 <= s < SLOTS:
                    out[rows(r * SLOTS + s), :] = made[rows(r), rows(i)].astype(BF16)
    deal(place, out, pieces, carried(sums[...]))


def second_square(place, labels_own, labels_other, sums, ham, *refs, order):
    near, sq, near_sq = refs[:4], refs[4], refs[5:9]
    density, answers, right, blocks = refs[9:]
    side = place[0]
    total = sums[...] + brought(near_sq[0]) + brought(near_sq[1]) + brought(near_sq[2])
    average = total[0:1, :] / order
    spread = jnp.sqrt(total[1:2, :] / order - average * average + 1e-06)
    lift = 0.5 + average / (4.0 * spread)
    scaling = 1.0 / (4.0 * spread)
    unit, linear, quadratic = lift * lift, 2.0 * lift * scaling, scaling * scaling
    eye = lax.broadcasted_iota(jnp.int32, (BW, BW), 0) == lax.broadcasted_iota(
        jnp.int32, (BW, BW), 1
    )
    unit_block = jnp.where(eye, jnp.broadcast_to(unit, (BW, BW)), 0.0)
    squares = {id(ham): sq} | {id(h): g for h, g in zip(near, near_sq)}
    masks = {}
    for piece in (ham, *near):
        masks[id(piece)] = piece[piece.shape[0] - META :, :].astype(F32)

    def make(piece, i, b, s):
        line = b % 2 * SLOTS + s
        value = quadratic * squares[id(piece)][rows(i), :].astype(F32)
        value = value - linear * piece[rows(i), :].astype(F32)
        if s == HALF:
            value = value + unit_block
        return (value * masks[id(piece)][line : line + 1, :]).astype(BF16)

    fill(place, right, ham, near, make)
    mask = masks[id(ham)]
    for j, made in square_pair(right):
        for i in range(3):
            for r in range(2):
                s = 3 * j + i - r
                if 0 <= s < SLOTS:
                    k = r * SLOTS + s
                    first = right[rows(HALF + r), rows(3 * j + i)].astype(F32)
                    value = (2.0 * first - made[rows(r), rows(i)]) * mask[k : k + 1, :]
                    blocks[k] = value.astype(BF16)
    for s in range(SLOTS):
        density[:, rows(s)] = blocks[side * SLOTS + s]
    for labels, row in ((labels_own, side), (labels_other, 1 - side)):
        for i in range(2 * answers.shape[0]):
            label = jnp.maximum(labels[i], 1)
            at = pl.multiple_of((row * 2 + i % 2) * BW, BW)
            answers[i // 2, pl.ds(at, BW), :] = blocks[row * SLOTS + label - 1]


def on_grid(pos, returned, prow, pcol, out):
    batches, points, _ = prow.shape
    lane = lax.broadcasted_iota(jnp.int32, (points, BW), 1)
    values = jnp.zeros((points, BW), F32)
    for b in range(batches):
        at = pl.multiple_of(pos[b] % 4 * BW, BW)
        block = returned[pos[b] // 4, pl.ds(at, BW), :]
        partial = jnp.dot(prow[b], block, preferred_element_type=F32) * pcol[b].astype(F32)
        values = jnp.where(lane == b, jnp.sum(partial, axis=1, keepdims=True), values)
    out[...] = values.T[:batches, :]


def exchanged(pieces):
    count = lax.axis_size(LINE)
    got = []
    for piece, step, turn in zip(pieces, (1, 1, 2, 2), (0, 1, 0, 1)):
        hops = [(i, (i + step) % count) for i in range(count) if i // step % 2 == turn]
        got.append(lax.ppermute(piece, LINE, hops + [(b, a) for a, b in hops]))
    return got


def added_over(sums, *rounds):
    for axis, step in rounds:
        size = lax.axis_size(axis)
        if step < size:
            sums = sums + lax.ppermute(sums, axis, [(i, i ^ step) for i in range(size)])
    return sums


ROUNDS = (
    (("layer", 1), ("layer", 2), ("layer", 4), ("ring", 4)),
    (("row", 1), ("row", 2), ("row", 4)),
)


def shards(phi_row, phi_col, weights, batch_route, batch_slot, ham_pattern, dens_pattern):
    batches, points, _ = phi_row.shape
    dests = lax.axis_size("ring")
    pairs = lax.axis_size(LINE)
    side = lax.axis_index("side")
    place = jnp.stack([side, lax.axis_index(LINE)]).astype(jnp.int32)
    depth = 2 * BW + META

    def shape(*dims, kind=BF16):
        return jax.ShapeDtypeStruct(dims, kind)

    out_other, out_own, position = call(
        integrate,
        (shape(dests, depth, BW), shape(dests, depth, BW), shape(batches, kind=jnp.int32)),
        [SMEM, SMEM, SMEM, VMEM, VMEM, VMEM],
        (VMEM, VMEM, SMEM),
        [
            pltpu.VMEM((batches, BW, BW), BF16),
            pltpu.SMEM((2 * dests,), jnp.int32),
        ],
        flops=2 * batches * points * BW * BW,
        moved=6 << 20,
    )(place, batch_route.reshape(batches), batch_slot, weights, phi_row, phi_col)

    def received(outgoing, parity, kind):
        arrived = lax.all_to_all(outgoing, "ring", split_axis=0, concat_axis=0, tiled=True)
        labels = arrived[:, 2 * BW : 2 * BW + 4, 0].astype(jnp.int32)
        labels = jnp.where(parity == 0, labels[:, :2], labels[:, 2:]).reshape(2 * dests)
        part = call(
            accumulate,
            shape(SLOTS * BW, BW, kind=kind),
            [SMEM, VMEM],
            VMEM,
            [pltpu.VMEM((SLOTS, BW, BW), F32)],
            moved=2 << 20,
        )(labels, arrived)
        return labels, part

    swap = [(0, 1), (1, 0)]
    labels_other, for_other = received(out_other, 1 - side, BF16)
    from_other = lax.ppermute(for_other, "side", swap)
    labels_own, part = received(out_own, side, F32)

    row_shape = shape(SLOTS * BW + META, BW)
    sums_shape = shape(SLOTS, BW, kind=F32)
    ham_own, sums = call(
        functools.partial(combine, pairs=pairs),
        (row_shape, sums_shape),
        [SMEM, SMEM, SMEM, VMEM, VMEM],
        (VMEM, VMEM),
        moved=2 << 20,
    )(place, ham_pattern, dens_pattern, part, from_other)
    sums = added_over(sums, *ROUNDS[0])
    held = call(hold, shape(SLOTS * BW + META + CARRIED, BW), [VMEM, VMEM], VMEM, moved=1 << 19)(
        sums, ham_own
    )
    ham_other = lax.ppermute(held, "side", swap)

    sizes = [len(REACH[t]) * BW for t in (-1, -1, -2, -2)]
    ham, *pieces, sums = call(
        spread,
        (shape(2 * SLOTS * BW + META, BW),)
        + tuple(shape(n + META, BW) for n in sizes)
        + (sums_shape,),
        [SMEM, VMEM, VMEM, VMEM],
        (VMEM,) * 6,
        moved=4 << 20,
    )(place, sums, ham_own, ham_other)
    near = exchanged(pieces)
    sums = added_over(sums, *ROUNDS[1])

    sq, *pieces = call(
        first_square,
        (shape(2 * SLOTS * BW, BW),) + tuple(shape(n + CARRIED, BW) for n in sizes),
        [SMEM] + [VMEM] * 6,
        (VMEM,) * 5,
        [pltpu.VMEM((WIDE, WIDE), BF16)],
        flops=4 * BW * WIDE * WIDE,
        moved=4 << 20,
    )(place, sums, ham, *near)
    near_sq = exchanged(pieces)

    density, answers = call(
        functools.partial(second_square, order=2 * pairs * BW),
        (shape(BW, SLOTS * BW), shape(dests, 4 * BW, BW)),
        [SMEM] * 3 + [VMEM] * 11,
        (VMEM, VMEM),
        [pltpu.VMEM((WIDE, WIDE), BF16), pltpu.VMEM((2 * SLOTS, BW, BW), BF16)],
        flops=4 * BW * WIDE * WIDE,
        moved=6 << 20,
    )(place, labels_own, labels_other, sums, ham, *near, sq, *near_sq)
    returned = lax.all_to_all(answers, "ring", split_axis=0, concat_axis=0, tiled=True)

    grid_density = call(
        on_grid,
        shape(batches, points, kind=F32),
        [SMEM, VMEM, VMEM, VMEM],
        VMEM,
        flops=2 * batches * points * BW * BW,
        moved=6 << 20,
    )(position, returned, phi_row, phi_col)
    return (density, grid_density)


def solution(mesh):
    layer, row, col = (mesh.shape[a] for a in ("layer", "row", "col"))
    split = Mesh(
        mesh.devices.reshape(layer, row, col // 2, 2), ("layer", "row", "ring", "side")
    )
    axes = ("layer", "row", "ring", "side")
    in_specs = (
        P(axes, None, None),
        P(axes, None, None),
        P(axes, None),
        P(axes, None),
        P(axes),
        P(axes, None),
        P(axes, None),
    )
    out_specs = (P(axes, None), P(axes, None))
    return jax.shard_map(
        shards, mesh=split, in_specs=in_specs, out_specs=out_specs, check_vma=False
    )
```
